32 devices in a mesh: parts: 1, node: 4 (over y, x), local: 8 (over z, core).
Axes of the slice: x: 2, y: 2, z: 4, core: 2. Of those that a mesh axis runs over, the one named last changes fastest.
Arguments:
- tokens: bfloat16 [2048, 4096], P(('parts', 'node', 'local')), may hold values from -6 to 6
- expert_ids: int32 [2048, 8], P(('parts', 'node', 'local')), may hold values from 0 to 15, all different within a row; in each aligned block of 64 rows (0 to 63, 64 to 127, ...) at most 40 rows name the same one
- gate_weights: float32 [2048, 8], P(('parts', 'node', 'local')), may hold values from 0.02 to 0.5
- w_gate: bfloat16 [4096, 12288], P(None, ('parts', 'node', 'local')), may hold values from -0.09375 to 0.09375
- w_up: bfloat16 [4096, 12288], P(None, ('parts', 'node', 'local')), may hold values from -0.09375 to 0.09375
- w_down: bfloat16 [12288, 4096], P(('parts', 'node', 'local')), may hold values from -0.21875 to 0.21875
Outputs:
- mixed: bfloat16 [2048, 4096], P(('parts', 'node', 'local'))
The draws below stay inside these ranges and needn't reach their ends.
Inputs may be any that keep to these rules, and one draw needn't show every extreme that they name: `expert_ids`: each token names 8 different experts; among the 64 tokens of one device no expert is named more than 40 times, and in some such block one expert is named exactly 40 times.
All inputs are finite; a program needn't handle non-finite values.
Results may differ from the reference program's by a relative error of at most 0.0058.
Values may be sent and summed in bfloat16 or wider, within the bound.
No kernel may reach another device: no remote copies, remote signals or barrier semaphores. Data moves between devices by JAX's collectives and lax.ppermute only.
A program may use at most 128 MiB of HBM per device.

```python
import math
import jax
import jax.numpy as jnp
import numpy as np
from jax import lax

D = 4096
FF = 768
TOPK = 8
TOK_DEV = 64
EXPERTS = 16
CAP = 40
TOKENS = 2048


def levels(stream_key, extent, pieces, smallest, top_value):
    level = 1.0
    for dim, blocks in pieces:
        steps = jax.random.uniform(jax.random.fold_in(jax.random.fold_in(stream_key, 6), dim), (blocks,), jnp.float32, smallest / len(pieces), top_value / len(pieces))
        level = level * jnp.repeat(jnp.exp(steps), extent[dim] // blocks).reshape((-1,) + (1,) * (len(extent) - 1 - dim))
    return level


def routed_block(stream_key, own, number, rows, number_of, top, reach, skew):
    order = jax.random.permutation(stream_key, number_of)
    packed, usual = portions_of(number_of, rows * top, reach, skew, True), portions_of(number_of, rows * top, reach, skew, False)
    places = jnp.arange(number_of)

    def named(tallies, rotation):
        used = int((tallies > 0).sum())
        fixed = max(1, used // 4)
        passed = fixed + (places - fixed + rotation * (used - fixed)) % max(1, number_of - fixed)
        return jnp.zeros((number_of,), jnp.int32).at[order[jnp.where(places < fixed, places, passed)]].set(jnp.asarray(tallies, jnp.int32))

    tallies = jnp.where(number % 4 == 0, named(packed, number // 4), named(usual, number - number // 4 - 1))
    mixed = jax.random.permutation(jax.random.fold_in(own, 3), number_of)
    donor, receiver = mixed[0:number_of // 2 * 2:2], mixed[1:number_of // 2 * 2:2]
    margin = jnp.minimum(tallies[donor] - 1, reach - tallies[receiver]) // 2
    margin = jnp.where((donor == order[0]) | (receiver == order[0]) | (tallies[receiver] == 0), 0, jnp.maximum(margin, 0))
    passed = jax.random.randint(jax.random.fold_in(own, 4), (number_of // 2,), 0, 1 << 20) % (margin + 1)
    tallies = tallies.at[donor].add(-passed).at[receiver].add(passed)
    labels = jnp.searchsorted(jnp.cumsum(tallies), jnp.arange(rows * top), side="right").astype(jnp.int32)
    grid = labels.reshape(top, rows).T
    grid = grid[jax.random.permutation(jax.random.fold_in(own, 1), rows)]
    rotation = jax.random.randint(jax.random.fold_in(own, 2), (rows, 1), 0, top)
    return jnp.take_along_axis(grid, (jnp.arange(top)[None, :] + rotation) % top, axis=1)


def portions_of(amount, total, bound, skew, full):
    loads = [(1 << 20) // math.isqrt(standing ** skew) + 1 for standing in range(1, amount + 1)]
    largest = bound if full else min(bound, max(-(-total // amount), total * loads[0] // sum(loads)))
    least = 1 if total - largest >= amount - 1 else 0
    holding, spare = [largest] + [least] * (amount - 1), total - largest - least * (amount - 1)
    while spare > 0:
        movable = [i for i in range(1, amount) if holding[i] < largest] or [i for i in range(1, amount) if holding[i] < bound]
        whole, left = sum([loads[i] for i in movable]), spare
        for i in movable:
            more = min(bound - holding[i], max(1, left * loads[i] // whole), spare)
            holding[i] = holding[i] + more
            spare = spare - more
    return np.array(holding)


def gaussian(key, shape, width, reach, split=(), held_as=jnp.bfloat16):
    loudness = levels(key, shape, split, -0.22, 0.18) if split else 1.0
    array = jax.random.normal(key, shape, jnp.float32) * width * loudness
    return jnp.minimum(jnp.maximum(array, -reach), reach).astype(held_as)


def setup_inputs(seed: int = 0, part: int = 0) -> dict:
    streams_of = jax.random.split(jax.random.key(seed), 7)
    part_keys = jax.random.split(jax.random.fold_in(streams_of[6], part), 7)
    tokens = gaussian(part_keys[0], (TOKENS, D), 1.0, 6.0, ((0, 32),))
    expert_ids_keys = jax.random.split(jax.random.fold_in(part_keys[1], 1), TOKENS // TOK_DEV)
    expert_ids_turns = jax.random.permutation(jax.random.fold_in(part_keys[1], 3), TOKENS // TOK_DEV)
    expert_ids = jax.vmap(lambda own, number: routed_block(jax.random.fold_in(part_keys[1], 2), own, number, TOK_DEV, EXPERTS, TOPK, CAP, 2))(expert_ids_keys, expert_ids_turns).reshape((TOKENS, TOPK))
    gate_weights = jnp.clip(jnp.exp(math.log(0.5) - 3.218876 * jax.random.uniform(part_keys[2], (TOKENS, TOPK), jnp.float32) ** levels(part_keys[2], (TOKENS, TOPK), ((0, 32),), -0.2, 0.2)), 0.02, 0.5)
    w_gate = gaussian(part_keys[3], (D, EXPERTS * FF), D ** -0.5, 0.09375, ((1, 32),))
    w_up = gaussian(part_keys[4], (D, EXPERTS * FF), D ** -0.5, 0.09375, ((1, 32),))
    w_down = gaussian(part_keys[5], (EXPERTS * FF, D), FF ** -0.5, 0.21875, ((0, 32),))
    return dict(tokens=tokens, expert_ids=expert_ids, gate_weights=gate_weights, w_gate=w_gate, w_up=w_up, w_down=w_down)


def reference(tokens, expert_ids, gate_weights, w_gate, w_up, w_down):
    groups = TOKENS // TOK_DEV
    pairs = TOK_DEV * TOPK
    block_ids = expert_ids.reshape(groups, pairs)
    one_hot = (block_ids[:, :, None] == jnp.arange(EXPERTS, dtype=jnp.int32)[None, None, :]).astype(jnp.int32)
    earlier = jnp.cumsum(one_hot, axis=1) - one_hot
    slot_rank = jnp.sum(earlier * one_hot, axis=2).astype(jnp.int32)
    token_index = jnp.broadcast_to(jnp.arange(TOKENS, dtype=jnp.int32).reshape(groups, TOK_DEV, 1), (groups, TOK_DEV, TOPK)).reshape(groups, pairs)
    block_index = jnp.broadcast_to(jnp.arange(groups, dtype=jnp.int32)[:, None], (groups, pairs))
    table = jnp.zeros((EXPERTS, groups, CAP), jnp.int32).at[block_ids, block_index, slot_rank].set(token_index)
    filled = jnp.zeros((EXPERTS, groups, CAP), jnp.float32).at[block_ids, block_index, slot_rank].set(1.0)

    def expert_out(expert):
        rows = tokens[table[expert].reshape(-1)]
        rows = (rows.astype(jnp.float32) * filled[expert].reshape(-1, 1)).astype(jnp.bfloat16)
        start = (expert * FF).astype(jnp.int32)
        gate_cols = lax.dynamic_slice_in_dim(w_gate, start, FF, 1)
        up_cols = lax.dynamic_slice_in_dim(w_up, start, FF, 1)
        down_rows = lax.dynamic_slice_in_dim(w_down, start, FF, 0)
        gate = jnp.dot(rows, gate_cols, preferred_element_type=jnp.float32)
        upper = jnp.dot(rows, up_cols, preferred_element_type=jnp.float32)
        hidden = (jax.nn.silu(gate) * upper).astype(jnp.bfloat16)
        return jnp.dot(hidden, down_rows, preferred_element_type=jnp.float32).astype(jnp.bfloat16)

    outputs = lax.map(expert_out, jnp.arange(EXPERTS, dtype=jnp.int32))

    def combine(block):
        chosen_ids = lax.dynamic_index_in_dim(block_ids, block, 0, keepdims=False)
        ranks = lax.dynamic_index_in_dim(slot_rank, block, 0, keepdims=False)
        chosen = outputs[chosen_ids, block * CAP + ranks].reshape(TOK_DEV, TOPK, D)
        weights = lax.dynamic_slice_in_dim(gate_weights, (block * TOK_DEV).astype(jnp.int32), TOK_DEV, 0)
        return jnp.sum(weights[:, :, None] * chosen.astype(jnp.float32), axis=1).astype(jnp.bfloat16)

    mixed = lax.map(combine, jnp.arange(groups, dtype=jnp.int32))
    return mixed.reshape(TOKENS, D)
```

```python
import functools

import jax
import jax.numpy as jnp
from jax import lax
from jax.experimental import pallas as pl
from jax.experimental.pallas import tpu as pltpu
from jax.sharding import PartitionSpec as P

LANES = 128
VMEM_BYTES = 50 * 2**20


def swap(value, axis, mask):
    pairs = [(source, source ^ mask) for source in range(lax.axis_size(axis))]
    return lax.ppermute(value, axis, pairs)


def pack_block(tokens, expert_ids, gate_weights):
    parts = [expert_ids.astype(jnp.float32)]
    rest = gate_weights
    for _ in range(3):
        piece = lax.reduce_precision(rest, exponent_bits=8, mantissa_bits=7)
        parts.append(piece)
        rest = rest - piece
    meta = jnp.concatenate(parts, axis=1).astype(jnp.bfloat16)
    meta = jnp.pad(meta, ((0, 0), (0, -meta.shape[1] % LANES)))
    return jnp.concatenate([tokens, meta], axis=1)


def slots(place, meta, top, chain, capacity, count):
    rows = meta.shape[0]
    node, link = place[0], place[1]
    lane = lax.broadcasted_iota(jnp.int32, (rows, LANES), 1)
    expert = (jnp.bitwise_xor(lane, node) * chain + link).astype(jnp.float32)
    chosen = jnp.zeros((rows, LANES), jnp.float32)
    weight = jnp.zeros((rows, LANES), jnp.float32)
    for k in range(top):
        hit = meta[:, k : k + 1] == expert
        gate = meta[:, top + k : top + k + 1] + meta[:, 2 * top + k : 2 * top + k + 1]
        gate = gate + meta[:, 3 * top + k : 3 * top + k + 1]
        chosen = chosen + jnp.where(hit, 1.0, 0.0)
        weight = weight + jnp.where(hit, gate, 0.0)
    before = lax.broadcasted_iota(jnp.int32, (rows, rows), 0) > lax.broadcasted_iota(jnp.int32, (rows, rows), 1)
    rank = jnp.dot(
        jnp.where(before, 1.0, 0.0).astype(jnp.bfloat16),
        chosen.astype(jnp.bfloat16),
        preferred_element_type=jnp.float32,
    )
    rank = jnp.where(chosen > 0.5, rank, -1.0)
    slot = lax.broadcasted_iota(jnp.int32, (rows, capacity), 1).astype(jnp.float32)
    return [(jnp.where(rank[:, n : n + 1] == slot, 1.0, 0.0), weight[:, n : n + 1]) for n in range(count)]


def select_kernel(top, chain, capacity, place, block, *outs):
    width = outs[0].shape[1]
    meta = block[:, width:].astype(jnp.float32)
    hots = [hot for hot, _ in slots(place, meta, top, chain, capacity, len(outs))]
    tokens = block[:, :width]
    for hot, out in zip(hots, outs):
        picked = lax.dot_general(
            hot.astype(jnp.bfloat16), tokens, (((0,), (0,)), ((), ())), preferred_element_type=jnp.float32
        )
        out[...] = picked.astype(jnp.bfloat16)


def smem():
    return pl.BlockSpec(memory_space=pltpu.SMEM)


def vmem():
    return pl.BlockSpec(memory_space=pltpu.VMEM)


def select(place, block, width, top, chain, capacity, count):
    return pl.pallas_call(
        functools.partial(select_kernel, top, chain, capacity),
        out_shape=[jax.ShapeDtypeStruct((capacity, width), jnp.bfloat16)] * count,
        in_specs=[smem(), vmem()],
        out_specs=[vmem()] * count,
        compiler_params=pltpu.CompilerParams(vmem_limit_bytes=VMEM_BYTES),
        cost_estimate=pl.CostEstimate(flops=0, bytes_accessed=6 * block.size, transcendentals=0),
        name="select",
    )(place, block)


def expert_kernel(pieces, half, *refs):
    rows, (gate0, gate1, up0, up1, down0, down1) = refs[:pieces], refs[pieces : pieces + 6]
    outs, (x, total) = refs[pieces + 6 : -2], refs[-2:]
    step = pl.program_id(0)
    size = rows[0].shape[0]

    @pl.when(step == 0)
    def _():
        x[...] = jnp.concatenate([r[...].astype(jnp.float32) for r in rows], axis=0).astype(jnp.bfloat16)

    def part(gate, up, down, first):
        both = jnp.concatenate([gate[...], up[...]], axis=1)
        product = jnp.dot(x[...], both, preferred_element_type=jnp.float32)
        tile = gate.shape[1]
        g, u = product[:, :tile], product[:, tile:]
        hidden = (g / (1.0 + jnp.exp(-g)) * u).astype(jnp.bfloat16)
        out = jnp.dot(hidden, down[...], preferred_element_type=jnp.float32)

        @pl.when(step == 0)
        def _():
            total[...] = out

        @pl.when(step > 0)
        def _():
            total[...] += out

    @pl.when(step < half)
    def _():
        part(gate0, up0, down0, True)

    @pl.when(step >= half)
    def _():
        part(gate1, up1, down1, False)

    @pl.when(step == 2 * half - 1)
    def _():
        for i, out in enumerate(outs):
            out[...] = total[i * size : (i + 1) * size, :].astype(jnp.bfloat16)


def expert(rows, own, other):
    size, width = rows[0].shape
    count = size * len(rows)
    hidden = own[0].shape[1]
    tile = LANES
    half = hidden // tile
    first = lambda i: jnp.minimum(i, half - 1)
    second = lambda i: jnp.maximum(i - half, 0)
    column = lambda at: pl.BlockSpec((width, tile), lambda i: (0, at(i)))
    row = lambda at: pl.BlockSpec((tile, width), lambda i: (at(i), 0))
    whole = pl.BlockSpec((size, width), lambda i: (0, 0))
    return pl.pallas_call(
        functools.partial(expert_kernel, len(rows), half),
        grid=(2 * half,),
        out_shape=[jax.ShapeDtypeStruct((size, width), jnp.bfloat16)] * len(rows),
        in_specs=[whole] * len(rows)
        + [column(first), column(second), column(first), column(second), row(first), row(second)],
        out_specs=[whole] * len(rows),
        scratch_shapes=[pltpu.VMEM((count, width), jnp.bfloat16), pltpu.VMEM((count, width), jnp.float32)],
        compiler_params=pltpu.CompilerParams(vmem_limit_bytes=VMEM_BYTES),
        cost_estimate=pl.CostEstimate(
            flops=12 * count * width * hidden, bytes_accessed=12 * width * hidden + 4 * count * width, transcendentals=0
        ),
        name="expert",
    )(*rows, own[0], other[0], own[1], other[1], own[2], other[2])


def combine_kernel(top, chain, capacity, count, place, block, *refs):
    results, others, out = refs[:count], refs[count:-1], refs[-1]
    meta = block[...].astype(jnp.float32)
    total = None
    for other in others:
        value = other[...].astype(jnp.float32)
        total = value if total is None else total + value
    for (hot, weight), result in zip(slots(place, meta, top, chain, capacity, count), results):
        scaled = hot * weight
        high = scaled.astype(jnp.bfloat16)
        low = (scaled - high.astype(jnp.float32)).astype(jnp.bfloat16)
        value = result[...]
        piece = jnp.dot(high, value, preferred_element_type=jnp.float32)
        piece = piece + jnp.dot(low, value, preferred_element_type=jnp.float32)
        total = piece if total is None else total + piece
    out[...] = total.astype(jnp.bfloat16)


def combine(place, block, results, others, top, chain):
    capacity, width = results[0].shape
    rows = block.shape[0]
    lead = pl.BlockSpec((rows, LANES), lambda i: (0, width // LANES))
    whole = lambda shape: pl.BlockSpec(shape, lambda i: (0, 0))
    return pl.pallas_call(
        functools.partial(combine_kernel, top, chain, capacity, len(results)),
        grid=(1,),
        out_shape=jax.ShapeDtypeStruct((rows, width), jnp.bfloat16),
        in_specs=[smem(), lead] + [whole((capacity, width))] * len(results) + [whole((rows, width))] * len(others),
        out_specs=whole((rows, width)),
        compiler_params=pltpu.CompilerParams(vmem_limit_bytes=VMEM_BYTES),
        cost_estimate=pl.CostEstimate(
            flops=0, bytes_accessed=2 * width * (rows * (1 + len(others)) + capacity * len(results)), transcendentals=0
        ),
        name="combine",
    )(place, block, *results, *others)


def per_device(tokens, expert_ids, gate_weights, w_gate, w_up, w_down):
    nodes = lax.axis_size("node")
    chain = lax.axis_size("local") // 2
    rows, top = expert_ids.shape
    width = tokens.shape[1]
    capacity = rows * top * 5 // (4 * nodes * chain)
    capacity = -(-capacity // 8) * 8
    place = jnp.stack([lax.axis_index("node"), lax.axis_index("local") // 2]).astype(jnp.int32)

    packed = pack_block(tokens, expert_ids, gate_weights)
    blocks = [packed] + [swap(packed, "local", 2 * step) for step in range(1, chain)]
    own = (w_gate, w_up, w_down)
    other = tuple(swap(weight, "local", 1) for weight in own)

    groups = [[0]]
    while groups[-1][-1] + 1 < chain:
        start = groups[-1][-1] + 1
        groups.append(list(range(start, 2 * start)))
    back = {}
    for group in groups:
        arrived = []
        for step in group:
            picked = select(place, blocks[step], width, top, chain, capacity, nodes)
            arrived += [picked[0]] + [swap(picked[n], "node", n) for n in range(1, nodes)]
        results = expert(arrived, own, other)
        for i, step in enumerate(group):
            back[step] = results[i * nodes : (i + 1) * nodes]
    sums = []
    for step in list(range(1, chain)) + [0]:
        result = back[step]
        returned = [result[0]] + [swap(result[n], "node", n) for n in range(1, nodes)]
        if step:
            partial = combine(place, blocks[step], returned, [], top, chain)
            sums.append(swap(partial, "local", 2 * step))
    return combine(place, packed, returned, sums, top, chain)


def solution(mesh):
    spread = ("parts", "node", "local")
    placed = (P(spread, None), P(spread, None), P(spread, None), P(None, spread), P(None, spread), P(spread, None))
    return jax.shard_map(
        per_device, mesh=mesh, in_specs=placed, out_specs=P(spread, None), check_vma=False
    )
```

```python
import functools

import jax
import jax.numpy as jnp
from jax import lax
from jax.experimental import pallas as pl
from jax.experimental.pallas import tpu as pltpu
from jax.sharding import PartitionSpec as P

LANES = 128
ORDER = [(2,), (3,), (1,), (0,)]
VMEM_BYTES = 34 * 2**20


def swap(value, axis, mask):
    pairs = [(source, source ^ mask) for source in range(lax.axis_size(axis))]
    return lax.ppermute(value, axis, pairs)


def after(value, earlier):
    if not earlier:
        return value
    return lax.optimization_barrier((value, *earlier))[0]


def together(moved, arrived):
    values = lax.optimization_barrier((*moved, *arrived[1:]))
    return values[: len(moved)], [arrived[0], *values[len(moved) :]]


def meta_of(ids, gates):
    rows, top = ids.shape
    parts = [ids[...].astype(jnp.float32)]
    rest = gates[...]
    for _ in range(3):
        piece = rest.astype(jnp.bfloat16).astype(jnp.float32)
        parts.append(piece)
        rest = rest - piece
    lane = lax.broadcasted_iota(jnp.int32, (rows, LANES), 1)
    meta = jnp.zeros((rows, LANES), jnp.float32)
    for i, part in enumerate(parts):
        for k in range(top):
            meta = jnp.where(lane == i * top + k, part[:, k : k + 1], meta)
    return meta


def slots(place, meta, top, chain, capacity, count):
    meta = meta.astype(jnp.float32)
    rows = meta.shape[0]
    node, link = place[0], place[1]
    lane = lax.broadcasted_iota(jnp.int32, (rows, LANES), 1)
    expert = (jnp.bitwise_xor(lane, node) * chain + link).astype(jnp.float32)
    chosen = jnp.zeros((rows, LANES), jnp.float32)
    weight = jnp.zeros((rows, LANES), jnp.float32)
    for k in range(top):
        hit = meta[:, k : k + 1] == expert
        gate = meta[:, top + k : top + k + 1] + meta[:, 2 * top + k : 2 * top + k + 1]
        gate = gate + meta[:, 3 * top + k : 3 * top + k + 1]
        chosen = chosen + jnp.where(hit, 1.0, 0.0)
        weight = weight + jnp.where(hit, gate, 0.0)
    before = lax.broadcasted_iota(jnp.int32, (rows, rows), 0) > lax.broadcasted_iota(jnp.int32, (rows, rows), 1)
    rank = jnp.dot(
        jnp.where(before, 1.0, 0.0).astype(jnp.bfloat16),
        chosen.astype(jnp.bfloat16),
        preferred_element_type=jnp.float32,
    )
    rank = jnp.where(chosen > 0.5, rank, -1.0)
    slot = lax.broadcasted_iota(jnp.int32, (rows, capacity), 1).astype(jnp.float32)
    return [(jnp.where(rank[:, n : n + 1] == slot, 1.0, 0.0), weight[:, n : n + 1]) for n in range(count)]


def smem():
    return pl.BlockSpec(memory_space=pltpu.SMEM)


def vmem():
    return pl.BlockSpec(memory_space=pltpu.VMEM)


def call(kernel, name, place, inputs, outs, scratch=(), flops=0, stay=0):
    moved = sum(2 * v.size for v in inputs) + sum(2 * v.size for v in outs)
    return pl.pallas_call(
        kernel,
        out_shape=outs,
        in_specs=[smem()] + [vmem()] * (len(inputs) - stay) + [pl.BlockSpec(memory_space=pl.ANY)] * stay,
        out_specs=[vmem()] * len(outs),
        scratch_shapes=list(scratch),
        compiler_params=pltpu.CompilerParams(vmem_limit_bytes=VMEM_BYTES),
        cost_estimate=pl.CostEstimate(flops=flops, bytes_accessed=moved, transcendentals=0),
        name=name,
    )(place, *inputs)


def array(*shape):
    return jax.ShapeDtypeStruct(shape, jnp.bfloat16)


def pick(top, chain, capacity, place, meta, tokens, outs):
    for (hot, _), out in zip(slots(place, meta, top, chain, capacity, len(outs)), outs):
        rows = lax.dot_general(
            hot.astype(jnp.bfloat16), tokens, (((0,), (0,)), ((), ())), preferred_element_type=jnp.float32
        )
        out[...] = rows.astype(jnp.bfloat16)


def first_kernel(top, chain, capacity, place, tokens, ids, gates, packed, *outs):
    width = tokens.shape[1]
    meta = meta_of(ids, gates)
    pick(top, chain, capacity, place, meta, tokens[...], outs)
    packed[:, :width] = tokens[...]
    packed[:, width:] = meta.astype(jnp.bfloat16)


def select_kernel(top, chain, capacity, place, block, *outs):
    width = outs[0].shape[1]
    pick(top, chain, capacity, place, block[:, width:], block[:, :width], outs)


def expert_kernel(capacity, count, place, *refs):
    rows, weights, outs = refs[:count], refs[count : count + 6], refs[count + 6 : 2 * count + 6]
    refs = refs[2 * count + 6 :]
    x, hidden, held, sems = refs[0], refs[1], refs[2:8], refs[8]
    cuts = 2
    copies = []
    for i, (source, target) in enumerate(zip(weights, held)):
        step = source.shape[0] // cuts
        copies.append(
            [
                pltpu.make_async_copy(
                    source.at[pl.ds(c * step, step)], target.at[pl.ds(c * step, step)], sems.at[i * cuts + c]
                )
                for c in range(cuts)
            ]
        )
    order = [copies[i + j][c] for i in (0, 3) for c in range(cuts) for j in range(2)]
    order += [copies[i][c] for i in (2, 5) for c in range(cuts)]
    for copy in order:
        copy.start()
    x[...] = jnp.concatenate([ref[...].astype(jnp.float32) for ref in rows], axis=0).astype(jnp.bfloat16)
    size = hidden.shape[1] // 2
    depth = x.shape[1] // 4
    for i in range(2):
        product = None
        for k in range(0, x.shape[1], depth):
            for c in range(cuts):
                if k == c * (x.shape[1] // cuts):
                    copies[3 * i][c].wait()
                    copies[3 * i + 1][c].wait()
            both = jnp.concatenate([held[3 * i][k : k + depth, :], held[3 * i + 1][k : k + depth, :]], axis=1)
            term = jnp.dot(x[:, k : k + depth], both, preferred_element_type=jnp.float32)
            product = term if product is None else product + term
        gate, up = product[:, :size], product[:, size:]
        hidden[:, i * size : (i + 1) * size] = (gate / (1.0 + jnp.exp(-gate)) * up).astype(jnp.bfloat16)
    for i in (2, 5):
        for copy in copies[i]:
            copy.wait()
    tile = 512
    for start in range(0, x.shape[1], tile):
        result = jnp.dot(hidden[:, :size], held[2][:, start : start + tile], preferred_element_type=jnp.float32)
        result += jnp.dot(hidden[:, size:], held[5][:, start : start + tile], preferred_element_type=jnp.float32)
        for n, out in enumerate(outs):
            out[:, start : start + tile] = result[n * capacity : (n + 1) * capacity].astype(jnp.bfloat16)


def weigh(pairs, values):
    total = None
    for (hot, weight), value in zip(pairs, values):
        scaled = hot * weight
        high = scaled.astype(jnp.bfloat16)
        low = (scaled - high.astype(jnp.float32)).astype(jnp.bfloat16)
        for factor in (high, low):
            piece = jnp.dot(factor, value, preferred_element_type=jnp.float32)
            total = piece if total is None else total + piece
    return total


def combine_kernel(top, chain, capacity, count, place, block, *refs):
    results, others, out = refs[:count], refs[count:-1], refs[-1]
    width = out.shape[1]
    total = weigh(slots(place, block[:, width:], top, chain, capacity, count), [ref[...] for ref in results])
    for ref in others:
        total = total + ref[...].astype(jnp.float32)
    out[...] = total.astype(jnp.bfloat16)


def chain_pairs(pairs):
    return [(2 * source + core, 2 * target + core) for source, target in pairs for core in range(2)]


def per_device(tokens, expert_ids, gate_weights, w_gate, w_up, w_down):
    nodes = lax.axis_size("node")
    chain = lax.axis_size("local") // 2
    rows, top = expert_ids.shape
    width = tokens.shape[1]
    capacity = rows * top * 5 // (4 * nodes * chain)
    capacity = -(-capacity // 8) * 8
    spot = lax.axis_index("local") // 2
    place = jnp.stack([lax.axis_index("node"), spot]).astype(jnp.int32)
    sizes = (top, chain, capacity)
    relay = chain == 4
    middle = (spot == 1) | (spot == 2)
    inner, outward, inward = [(1, 2), (2, 1)], [(1, 0), (2, 3)], [(0, 1), (3, 2)]
    hop = lambda value, pairs: lax.ppermute(value, "local", chain_pairs(pairs))
    send = lambda values: [values[0]] + [swap(values[n], "node", n) for n in range(1, nodes)]

    packed, *picked = call(
        functools.partial(first_kernel, *sizes),
        "first",
        place,
        [tokens, expert_ids, gate_weights],
        [array(rows, width + LANES)] + [array(capacity, width)] * nodes,
    )
    arrived = {0: send(picked)}
    own = (w_gate, w_up, w_down)
    other = [swap(w_gate, "local", 1)]
    blocks = [packed]

    def pick_for(step, *token):
        block = after(blocks[step], token)
        picked = call(
            functools.partial(select_kernel, *sizes), "select", place, [block], [array(capacity, width)] * nodes
        )
        arrived[step] = send(picked)

    if relay:
        moved = [swap(packed, "local", 2), hop(after(packed, other), inner)]
        (first, third), arrived[0] = together(moved, arrived[0])
        blocks.append(first)
        pick_for(1)
        moved = [hop(first, inner), hop(third, outward)]
        moved, arrived[1] = together(moved, arrived[1])
        blocks.append(jnp.where(middle, *moved))
        pick_for(2)
        other.append(swap(after(w_up, blocks[2:]), "local", 1))
        (last_hop, other[1]), arrived[2] = together([hop(blocks[2], outward), other[1]], arrived[2])
        blocks.append(jnp.where(middle, third, last_hop))
        pick_for(3)
    else:
        for step in range(1, chain):
            blocks.append(swap(packed, "local", 2 * step))
            pick_for(step)
        other.append(swap(w_up, "local", 1))
    other.append(swap(after(w_down, [other[1], blocks[-1]]), "local", 1))

    def run(group):
        count = nodes * len(group)
        inputs = [value for step in group for value in arrived[step]]
        inputs[0] = after(inputs[0], last)
        outs = call(
            functools.partial(expert_kernel, capacity, count),
            "expert",
            place,
            [*inputs, *own, *other],
            [array(capacity, width)] * count,
            [
                pltpu.VMEM((count * capacity, width), jnp.bfloat16),
                pltpu.VMEM((count * capacity, 2 * w_gate.shape[1]), jnp.bfloat16),
            ]
            + [pltpu.VMEM(weight.shape, weight.dtype) for weight in own * 2]
            + [pltpu.SemaphoreType.DMA((12,))],
            flops=12 * count * capacity * width * w_gate.shape[1],
            stay=6,
        )
        last[:] = [outs[0]]
        for i, step in enumerate(group):
            results[step] = outs[i * nodes : (i + 1) * nodes]

    results, last = {}, []
    for group in ORDER if relay else [(step,) for step in range(chain)]:
        run(group)
    extra = {step: [] for step in range(chain)}
    kept = None
    for step in reversed(range(chain)):
        (total,) = call(
            functools.partial(combine_kernel, *sizes, nodes),
            "combine",
            place,
            [after(blocks[step], last), *send(results[step]), *extra[step]],
            [array(rows, width)],
        )
        last = [total]
        if relay and step == 3:
            kept = total
            extra[2].append(hop(total, inward))
        elif relay and step == 2:
            ends = hop(total, inward).astype(jnp.float32)
            kept = (kept.astype(jnp.float32) + ends).astype(jnp.bfloat16)
            extra[0].append(hop(kept, inner))
            extra[1].append(hop(total, inner))
        elif step:
            extra[0].append(swap(total, "local", 2 * step))
    return total


def solution(mesh):
    spread = ("parts", "node", "local")
    placed = (P(spread, None), P(spread, None), P(spread, None), P(None, spread), P(None, spread), P(spread, None))
    return jax.shard_map(
        per_device, mesh=mesh, in_specs=placed, out_specs=P(spread, None), check_vma=False
    )
```

```python
import functools

import jax
import jax.numpy as jnp
from jax import lax
from jax.experimental import pallas as pl
from jax.experimental.pallas import tpu as pltpu
from jax.sharding import PartitionSpec as P

LANES = 128
ORDER = [(2,), (3,), (1,), (0,)]
VMEM_BYTES, EXPERT_BYTES = 8 * 2**20, 44 * 2**20


def swap(value, axis, mask):
    pairs = [(source, source ^ mask) for source in range(lax.axis_size(axis))]
    return lax.ppermute(value, axis, pairs)


def after(value, earlier):
    if not earlier:
        return value
    return lax.optimization_barrier((value, *earlier))[0]


def together(moved, arrived):
    values = lax.optimization_barrier((*moved, *arrived[1:]))
    return values[: len(moved)], [arrived[0], *values[len(moved) :]]


def meta_of(ids, gates):
    parts = [ids[...].astype(jnp.float32)]
    rest = gates[...]
    for _ in range(3):
        piece = rest.astype(jnp.bfloat16).astype(jnp.float32)
        parts.append(piece)
        rest = rest - piece
    parts = jnp.concatenate(parts, axis=0).astype(jnp.bfloat16)
    count = parts.shape[0]
    same = lax.broadcasted_iota(jnp.int32, (count, LANES), 0) == lax.broadcasted_iota(jnp.int32, (count, LANES), 1)
    unit = jnp.where(same, 1.0, 0.0).astype(jnp.bfloat16)
    return lax.dot_general(parts, unit, (((0,), (0,)), ((), ())), preferred_element_type=jnp.float32)


def slots(place, meta, top, chain, capacity, count):
    meta = meta.astype(jnp.float32)
    rows = meta.shape[0]
    node, link = place[0], place[1]
    lane = lax.broadcasted_iota(jnp.int32, (rows, LANES), 1)
    expert = (jnp.bitwise_xor(lane, node) * chain + link).astype(jnp.float32)
    chosen = jnp.zeros((rows, LANES), jnp.float32)
    weight = jnp.zeros((rows, LANES), jnp.float32)
    for k in range(top):
        hit = meta[:, k : k + 1] == expert
        gate = meta[:, top + k : top + k + 1] + meta[:, 2 * top + k : 2 * top + k + 1]
        gate = gate + meta[:, 3 * top + k : 3 * top + k + 1]
        chosen = chosen + jnp.where(hit, 1.0, 0.0)
        weight = weight + jnp.where(hit, gate, 0.0)
    before = lax.broadcasted_iota(jnp.int32, (rows, rows), 0) > lax.broadcasted_iota(jnp.int32, (rows, rows), 1)
    rank = jnp.dot(
        jnp.where(before, 1.0, 0.0).astype(jnp.bfloat16),
        chosen.astype(jnp.bfloat16),
        preferred_element_type=jnp.float32,
    )
    rank = jnp.where(chosen > 0.5, rank, -1.0)
    slot = lax.broadcasted_iota(jnp.int32, (rows, capacity), 1).astype(jnp.float32)
    return [(jnp.where(rank[:, n : n + 1] == slot, 1.0, 0.0), weight[:, n : n + 1]) for n in range(count)]


def smem():
    return pl.BlockSpec(memory_space=pltpu.SMEM)


def vmem():
    return pl.BlockSpec(memory_space=pltpu.VMEM)


def call(kernel, name, place, inputs, outs, scratch=(), flops=0, stay=0):
    moved = sum(2 * v.size for v in inputs) + sum(2 * v.size for v in outs)
    return pl.pallas_call(
        kernel,
        out_shape=outs,
        in_specs=[smem()] + [vmem()] * (len(inputs) - stay) + [pl.BlockSpec(memory_space=pltpu.HBM)] * stay,
        out_specs=[vmem()] * len(outs),
        scratch_shapes=list(scratch),
        compiler_params=pltpu.CompilerParams(vmem_limit_bytes=EXPERT_BYTES if stay else VMEM_BYTES),
        cost_estimate=pl.CostEstimate(flops=flops, bytes_accessed=moved, transcendentals=0),
        name=name,
    )(place, *inputs)


def array(*shape):
    return jax.ShapeDtypeStruct(shape, jnp.bfloat16)


def pick(top, chain, capacity, place, meta, tokens, outs):
    for (hot, _), out in zip(slots(place, meta, top, chain, capacity, len(outs)), outs):
        rows = lax.dot_general(
            hot.astype(jnp.bfloat16), tokens, (((0,), (0,)), ((), ())), preferred_element_type=jnp.float32
        )
        out[...] = rows.astype(jnp.bfloat16)


def first_kernel(top, chain, capacity, place, tokens_from, ids_from, gates_from, packed, *refs):
    outs, (tokens, ids, gates, sems) = refs[:-4], refs[-4:]
    copies = [
        pltpu.make_async_copy(source, target, sems.at[i])
        for i, (source, target) in enumerate(((ids_from, ids), (gates_from, gates), (tokens_from, tokens)))
    ]
    for copy in copies:
        copy.start()
    copies[0].wait()
    copies[1].wait()
    width = tokens.shape[1]
    meta = meta_of(ids, gates)
    packed[:, width:] = meta.astype(jnp.bfloat16)
    copies[2].wait()
    packed[:, :width] = tokens[...]
    pick(top, chain, capacity, place, meta, tokens[...], outs)


def select_kernel(top, chain, capacity, inputs, place, *refs):
    block, outs = refs[0][...], refs[inputs:]
    width = outs[0].shape[1]
    if inputs == 2:
        block = jnp.where(place[2] == 1, block, refs[1][...])
        kept, outs = outs[-1], outs[:-1]
        kept[...] = block
    pick(top, chain, capacity, place, block[:, width:], block[:, :width], outs)


def expert_kernel(capacity, count, place, *refs):
    rows, weights, outs = refs[:count], refs[count : count + 6], refs[count + 6 : 2 * count + 6]
    refs = refs[2 * count + 6 :]
    x, hidden, held, sems = refs[0], refs[1], refs[2:8], refs[8]
    cuts = 2
    copies = []
    for i, (source, target) in enumerate(zip(weights, held)):
        step = source.shape[0] // cuts
        copies.append(
            [
                pltpu.make_async_copy(
                    source.at[pl.ds(c * step, step)], target.at[pl.ds(c * step, step)], sems.at[i * cuts + c]
                )
                for c in range(cuts)
            ]
        )
    order = [copies[i + j][c] for i in (0, 3) for c in range(cuts) for j in range(2)]
    order += [copies[i][c] for i in (2, 5) for c in range(cuts)]
    for copy in order:
        copy.start()
    x[...] = jnp.concatenate([ref[...].astype(jnp.float32) for ref in rows], axis=0).astype(jnp.bfloat16)
    size = hidden.shape[1] // 2
    depth = x.shape[1] // 4
    for i in range(2):
        product = None
        for k in range(0, x.shape[1], depth):
            for c in range(cuts):
                if k == c * (x.shape[1] // cuts):
                    copies[3 * i][c].wait()
                    copies[3 * i + 1][c].wait()
            both = jnp.concatenate([held[3 * i][k : k + depth, :], held[3 * i + 1][k : k + depth, :]], axis=1)
            term = jnp.dot(x[:, k : k + depth], both, preferred_element_type=jnp.float32)
            product = term if product is None else product + term
        gate, up = product[:, :size], product[:, size:]
        hidden[:, i * size : (i + 1) * size] = (gate / (1.0 + jnp.exp(-gate)) * up).astype(jnp.bfloat16)
    for i in (2, 5):
        for copy in copies[i]:
            copy.wait()
    tile = 512
    for start in range(0, x.shape[1], tile):
        result = jnp.dot(hidden[:, :size], held[2][:, start : start + tile], preferred_element_type=jnp.float32)
        result += jnp.dot(hidden[:, size:], held[5][:, start : start + tile], preferred_element_type=jnp.float32)
        for n, out in enumerate(outs):
            out[:, start : start + tile] = result[n * capacity : (n + 1) * capacity].astype(jnp.bfloat16)


def weigh(pairs, values):
    total = None
    for (hot, weight), value in zip(pairs, values):
        scaled = hot * weight
        high = scaled.astype(jnp.bfloat16)
        low = (scaled - high.astype(jnp.float32)).astype(jnp.bfloat16)
        for factor in (high, low):
            piece = jnp.dot(factor, value, preferred_element_type=jnp.float32)
            total = piece if total is None else total + piece
    return total


def combine_kernel(top, chain, capacity, count, place, block, *refs):
    results, others, out = refs[:count], refs[count:-1], refs[-1]
    width = out.shape[1]
    total = weigh(slots(place, block[:, width:], top, chain, capacity, count), [ref[...] for ref in results])
    for ref in others:
        total = total + ref[...].astype(jnp.float32)
    out[...] = total.astype(jnp.bfloat16)


def chain_pairs(pairs):
    return [(2 * source + core, 2 * target + core) for source, target in pairs for core in range(2)]


def per_device(tokens, expert_ids, gate_weights, w_gate, w_up, w_down):
    nodes = lax.axis_size("node")
    chain = lax.axis_size("local") // 2
    rows, top = expert_ids.shape
    width = tokens.shape[1]
    capacity = rows * top * 5 // (4 * nodes * chain)
    capacity = -(-capacity // 8) * 8
    spot = lax.axis_index("local") // 2
    middle = (spot == 1) | (spot == 2)
    place = jnp.stack([lax.axis_index("node"), spot, middle]).astype(jnp.int32)
    sizes = (top, chain, capacity)
    relay = chain == 4
    inner, outward, inward = [(1, 2), (2, 1)], [(1, 0), (2, 3)], [(0, 1), (3, 2)]
    hop = lambda value, pairs: lax.ppermute(value, "local", chain_pairs(pairs))
    send = lambda values: [values[0]] + [swap(values[n], "node", n) for n in range(1, nodes)]

    packed, *picked = call(
        functools.partial(first_kernel, *sizes),
        "first",
        place,
        [tokens, expert_ids.T, gate_weights.T],
        [array(rows, width + LANES)] + [array(capacity, width)] * nodes,
        [
            pltpu.VMEM((rows, width), tokens.dtype),
            pltpu.VMEM((top, rows), expert_ids.dtype),
            pltpu.VMEM((top, rows), gate_weights.dtype),
            pltpu.SemaphoreType.DMA((3,)),
        ],
        stay=3,
    )
    arrived = {0: send(picked)}
    own = (w_gate, w_up, w_down)
    other = [swap(w_gate, "local", 1)]
    blocks = [packed]

    def pick_for(step, *inputs):
        outs = [array(capacity, width)] * nodes + [array(*packed.shape)] * (len(inputs) - 1)
        picked = call(
            functools.partial(select_kernel, *sizes, len(inputs)), "select", place, list(inputs), outs
        )
        arrived[step] = send(picked[:nodes])
        blocks.append(picked[nodes] if len(inputs) > 1 else inputs[0])

    if relay:
        moved = [swap(packed, "local", 2), hop(after(packed, other), inner)]
        (first, third), arrived[0] = together(moved, arrived[0])
        pick_for(1, first)
        moved = [hop(first, inner), hop(third, outward)]
        moved, arrived[1] = together(moved, arrived[1])
        pick_for(2, *moved)
        other.append(swap(after(w_up, blocks[2:]), "local", 1))
        (last_hop, other[1]), arrived[2] = together([hop(blocks[2], outward), other[1]], arrived[2])
        pick_for(3, third, last_hop)
    else:
        for step in range(1, chain):
            pick_for(step, swap(packed, "local", 2 * step))
        other.append(swap(w_up, "local", 1))
    other.append(swap(after(w_down, [other[1], blocks[-1]]), "local", 1))

    def run(group):
        count = nodes * len(group)
        inputs = [value for step in group for value in arrived[step]]
        inputs[0] = after(inputs[0], last)
        outs = call(
            functools.partial(expert_kernel, capacity, count),
            "expert",
            place,
            [*inputs, *own, *other],
            [array(capacity, width)] * count,
            [
                pltpu.VMEM((count * capacity, width), jnp.bfloat16),
                pltpu.VMEM((count * capacity, 2 * w_gate.shape[1]), jnp.bfloat16),
            ]
            + [pltpu.VMEM(weight.shape, weight.dtype) for weight in own * 2]
            + [pltpu.SemaphoreType.DMA((12,))],
            flops=12 * count * capacity * width * w_gate.shape[1],
            stay=6,
        )
        last[:] = [outs[0]]
        for i, step in enumerate(group):
            results[step] = outs[i * nodes : (i + 1) * nodes]

    results, last = {}, []
    for group in ORDER if relay else [(step,) for step in range(chain)]:
        run(group)
    sums, totals = [], []
    for step in reversed(range(chain)):
        ready = [*totals[-2:-1], *sums[:-2]] if step < chain - 2 else []
        result = results[step]
        returned = send([result[0]] + [after(value, ready) for value in result[1:]])
        (total,) = call(
            functools.partial(combine_kernel, *sizes, nodes),
            "combine",
            place,
            [after(blocks[step], [*totals[-1:], *(results[0][:1] if step == chain - 2 else [])]), *returned, *([] if step else sums)],
            [array(rows, width)],
        )
        totals.append(total)
        if step:
            sums.append(swap(total, "local", 2 * step))
    return total


def solution(mesh):
    spread = ("parts", "node", "local")
    placed = (P(spread, None), P(spread, None), P(spread, None), P(None, spread), P(None, spread), P(spread, None))
    return jax.shard_map(
        per_device, mesh=mesh, in_specs=placed, out_specs=P(spread, None), check_vma=False
    )
```

```python
import functools

import jax
import jax.numpy as jnp
from jax import lax
from jax.experimental import pallas as pl
from jax.experimental.pallas import tpu as pltpu
from jax.sharding import PartitionSpec as P

LANES = 128
ORDER = [(2,), (3,), (1,), (0,)]
VMEM_BYTES, EXPERT_BYTES = 8 * 2**20, 26 * 2**20


def swap(value, axis, mask):
    pairs = [(source, source ^ mask) for source in range(lax.axis_size(axis))]
    return lax.ppermute(value, axis, pairs)


def after(value, earlier):
    if not earlier:
        return value
    return lax.optimization_barrier((value, *earlier))[0]


def together(moved, arrived):
    values = lax.optimization_barrier((*moved, *arrived[1:]))
    return values[: len(moved)], [arrived[0], *values[len(moved) :]]


def meta_of(ids, gates):
    parts = [ids[...].astype(jnp.float32)]
    rest = gates[...]
    for _ in range(3):
        piece = rest.astype(jnp.bfloat16).astype(jnp.float32)
        parts.append(piece)
        rest = rest - piece
    parts = jnp.concatenate(parts, axis=0).astype(jnp.bfloat16)
    count = parts.shape[0]
    same = lax.broadcasted_iota(jnp.int32, (count, LANES), 0) == lax.broadcasted_iota(jnp.int32, (count, LANES), 1)
    unit = jnp.where(same, 1.0, 0.0).astype(jnp.bfloat16)
    return lax.dot_general(parts, unit, (((0,), (0,)), ((), ())), preferred_element_type=jnp.float32)


def slots(place, meta, top, chain, capacity, count):
    meta = meta.astype(jnp.float32)
    rows = meta.shape[0]
    node, link = place[0], place[1]
    lane = lax.broadcasted_iota(jnp.int32, (rows, LANES), 1)
    expert = (jnp.bitwise_xor(lane, node) * chain + link).astype(jnp.float32)
    chosen = jnp.zeros((rows, LANES), jnp.float32)
    weight = jnp.zeros((rows, LANES), jnp.float32)
    for k in range(top):
        hit = meta[:, k : k + 1] == expert
        gate = meta[:, top + k : top + k + 1] + meta[:, 2 * top + k : 2 * top + k + 1]
        gate = gate + meta[:, 3 * top + k : 3 * top + k + 1]
        chosen = chosen + jnp.where(hit, 1.0, 0.0)
        weight = weight + jnp.where(hit, gate, 0.0)
    before = lax.broadcasted_iota(jnp.int32, (rows, rows), 0) > lax.broadcasted_iota(jnp.int32, (rows, rows), 1)
    rank = jnp.dot(
        jnp.where(before, 1.0, 0.0).astype(jnp.bfloat16),
        chosen.astype(jnp.bfloat16),
        preferred_element_type=jnp.float32,
    )
    rank = jnp.where(chosen > 0.5, rank, -1.0)
    slot = lax.broadcasted_iota(jnp.int32, (rows, capacity), 1).astype(jnp.float32)
    return [(jnp.where(rank[:, n : n + 1] == slot, 1.0, 0.0), weight[:, n : n + 1]) for n in range(count)]


def smem():
    return pl.BlockSpec(memory_space=pltpu.SMEM)


def vmem():
    return pl.BlockSpec(memory_space=pltpu.VMEM)


def call(kernel, name, place, inputs, outs, scratch=(), flops=0, stay=0):
    moved = sum(2 * v.size for v in inputs) + sum(2 * v.size for v in outs)
    return pl.pallas_call(
        kernel,
        out_shape=outs,
        in_specs=[smem()] + [vmem()] * (len(inputs) - stay) + [pl.BlockSpec(memory_space=pltpu.HBM)] * stay,
        out_specs=[vmem()] * len(outs),
        scratch_shapes=list(scratch),
        compiler_params=pltpu.CompilerParams(vmem_limit_bytes=EXPERT_BYTES if flops else VMEM_BYTES),
        cost_estimate=pl.CostEstimate(flops=flops, bytes_accessed=moved, transcendentals=0),
        name=name,
    )(place, *inputs)


def array(*shape):
    return jax.ShapeDtypeStruct(shape, jnp.bfloat16)


def pick(top, chain, capacity, place, meta, tokens, outs):
    for (hot, _), out in zip(slots(place, meta, top, chain, capacity, len(outs)), outs):
        rows = lax.dot_general(
            hot.astype(jnp.bfloat16), tokens, (((0,), (0,)), ((), ())), preferred_element_type=jnp.float32
        )
        out[...] = rows.astype(jnp.bfloat16)


def first_kernel(top, chain, capacity, place, tokens_from, ids_from, gates_from, packed, *refs):
    outs, (tokens, ids, gates, sems) = refs[:-4], refs[-4:]
    copies = [
        pltpu.make_async_copy(source, target, sems.at[i])
        for i, (source, target) in enumerate(((ids_from, ids), (gates_from, gates), (tokens_from, tokens)))
    ]
    for copy in copies:
        copy.start()
    copies[0].wait()
    copies[1].wait()
    width = tokens.shape[1]
    meta = meta_of(ids, gates)
    packed[:, width:] = meta.astype(jnp.bfloat16)
    copies[2].wait()
    packed[:, :width] = tokens[...]
    pick(top, chain, capacity, place, meta, tokens[...], outs)


def select_kernel(top, chain, capacity, inputs, place, *refs):
    block, outs = refs[0][...], refs[inputs:]
    width = outs[0].shape[1]
    if inputs == 2:
        block = jnp.where(place[2] == 1, block, refs[1][...])
        kept, outs = outs[-1], outs[:-1]
        kept[...] = block
    pick(top, chain, capacity, place, block[:, width:], block[:, :width], outs)


def expert_kernel(capacity, count, place, *refs):
    rows, weights, outs = refs[:count], refs[count : count + 6], refs[count + 6 : 2 * count + 6]
    refs = refs[2 * count + 6 :]
    x, hidden, held, sems = refs[0], refs[1], [*weights[:3], *refs[2:5]], refs[5]
    cuts = 2
    copies = []
    for i, (source, target) in enumerate(zip(weights[3:], held[3:])):
        step = source.shape[0] // cuts
        copies.append(
            [
                pltpu.make_async_copy(
                    source.at[pl.ds(c * step, step)], target.at[pl.ds(c * step, step)], sems.at[i * cuts + c]
                )
                for c in range(cuts)
            ]
        )
    order = [copies[i][c] for c in range(cuts) for i in range(2)] + copies[2]
    for copy in order:
        copy.start()
    x[...] = jnp.concatenate([ref[...].astype(jnp.float32) for ref in rows], axis=0).astype(jnp.bfloat16)
    size = hidden.shape[1] // 2
    depth = x.shape[1] // 4
    for i in range(2):
        product = None
        for k in range(0, x.shape[1], depth):
            for c in range(cuts):
                if i == 1 and k == c * (x.shape[1] // cuts):
                    copies[0][c].wait()
                    copies[1][c].wait()
            both = jnp.concatenate([held[3 * i][k : k + depth, :], held[3 * i + 1][k : k + depth, :]], axis=1)
            term = jnp.dot(x[:, k : k + depth], both, preferred_element_type=jnp.float32)
            product = term if product is None else product + term
        gate, up = product[:, :size], product[:, size:]
        hidden[:, i * size : (i + 1) * size] = (gate / (1.0 + jnp.exp(-gate)) * up).astype(jnp.bfloat16)
    for copy in copies[2]:
        copy.wait()
    tile = 512
    for start in range(0, x.shape[1], tile):
        result = jnp.dot(hidden[:, :size], held[2][:, start : start + tile], preferred_element_type=jnp.float32)
        result += jnp.dot(hidden[:, size:], held[5][:, start : start + tile], preferred_element_type=jnp.float32)
        for n, out in enumerate(outs):
            out[:, start : start + tile] = result[n * capacity : (n + 1) * capacity].astype(jnp.bfloat16)


def weigh(pairs, values):
    total = None
    for (hot, weight), value in zip(pairs, values):
        scaled = hot * weight
        high = scaled.astype(jnp.bfloat16)
        low = (scaled - high.astype(jnp.float32)).astype(jnp.bfloat16)
        both = jnp.dot(jnp.concatenate([high, low], axis=0), value, preferred_element_type=jnp.float32)
        piece = both[: hot.shape[0]] + both[hot.shape[0] :]
        total = piece if total is None else total + piece
    return total


def combine_kernel(top, chain, capacity, count, place, block, *refs):
    results, others, out = refs[:count], refs[count:-1], refs[-1]
    width = out.shape[1]
    total = weigh(slots(place, block[:, width:], top, chain, capacity, count), [ref[...] for ref in results])
    for ref in others:
        total = total + ref[...].astype(jnp.float32)
    out[...] = total.astype(jnp.bfloat16)


def chain_pairs(pairs):
    return [(2 * source + core, 2 * target + core) for source, target in pairs for core in range(2)]


def per_device(tokens, expert_ids, gate_weights, w_gate, w_up, w_down):
    nodes = lax.axis_size("node")
    chain = lax.axis_size("local") // 2
    rows, top = expert_ids.shape
    width = tokens.shape[1]
    capacity = rows * top * 5 // (4 * nodes * chain)
    capacity = -(-capacity // 8) * 8
    spot = lax.axis_index("local") // 2
    middle = (spot == 1) | (spot == 2)
    place = jnp.stack([lax.axis_index("node"), spot, middle]).astype(jnp.int32)
    sizes = (top, chain, capacity)
    relay = chain == 4
    inner, outward, inward = [(1, 2), (2, 1)], [(1, 0), (2, 3)], [(0, 1), (3, 2)]
    hop = lambda value, pairs: lax.ppermute(value, "local", chain_pairs(pairs))
    send = lambda values: [values[0]] + [swap(values[n], "node", n) for n in range(1, nodes)]

    packed, *picked = call(
        functools.partial(first_kernel, *sizes),
        "first",
        place,
        [tokens, expert_ids.T, gate_weights.T],
        [array(rows, width + LANES)] + [array(capacity, width)] * nodes,
        [
            pltpu.VMEM((rows, width), tokens.dtype),
            pltpu.VMEM((top, rows), expert_ids.dtype),
            pltpu.VMEM((top, rows), gate_weights.dtype),
            pltpu.SemaphoreType.DMA((3,)),
        ],
        stay=3,
    )
    arrived = {0: send(picked)}
    own = (w_gate, w_up, w_down)
    other = [swap(w_gate, "local", 1)]
    blocks = [packed]

    def pick_for(step, *inputs):
        outs = [array(capacity, width)] * nodes + [array(*packed.shape)] * (len(inputs) - 1)
        picked = call(
            functools.partial(select_kernel, *sizes, len(inputs)), "select", place, list(inputs), outs
        )
        arrived[step] = send(picked[:nodes])
        blocks.append(picked[nodes] if len(inputs) > 1 else inputs[0])

    if relay:
        moved = [swap(packed, "local", 2), hop(after(packed, other), inner)]
        (first, third), arrived[0] = together(moved, arrived[0])
        pick_for(1, first)
        moved = [hop(first, inner), hop(third, outward)]
        moved, arrived[1] = together(moved, arrived[1])
        pick_for(2, *moved)
        other.append(swap(after(w_up, blocks[2:]), "local", 1))
        (last_hop, other[1]), arrived[2] = together([hop(blocks[2], outward), other[1]], arrived[2])
        pick_for(3, third, last_hop)
    else:
        for step in range(1, chain):
            pick_for(step, swap(packed, "local", 2 * step))
        other.append(swap(w_up, "local", 1))
    other.append(swap(after(w_down, [other[1], blocks[-1]]), "local", 1))

    def run(group):
        count = nodes * len(group)
        inputs = [value for step in group for value in arrived[step]]
        inputs[0] = after(inputs[0], last)
        outs = call(
            functools.partial(expert_kernel, capacity, count),
            "expert",
            place,
            [*inputs, *own, *other],
            [array(capacity, width)] * count,
            [
                pltpu.VMEM((count * capacity, width), jnp.bfloat16),
                pltpu.VMEM((count * capacity, 2 * w_gate.shape[1]), jnp.bfloat16),
            ]
            + [pltpu.VMEM(weight.shape, weight.dtype) for weight in own]
            + [pltpu.SemaphoreType.DMA((6,))],
            flops=12 * count * capacity * width * w_gate.shape[1],
            stay=3,
        )
        last[:] = [outs[0]]
        for i, step in enumerate(group):
            results[step] = outs[i * nodes : (i + 1) * nodes]

    results, last = {}, []
    for group in ORDER if relay else [(step,) for step in range(chain)]:
        run(group)
    sums, totals = [], []
    for step in reversed(range(chain)):
        ready = [*totals[:1], *(sums[:1] if step == 0 else [])] if step < chain - 2 else []
        result = results[step]
        returned = send([result[0]] + [after(value, ready) for value in result[1:]])
        (total,) = call(
            functools.partial(combine_kernel, *sizes, nodes),
            "combine",
            place,
            [after(blocks[step], [*totals[-1:], *(results[0][:1] if step == chain - 2 else [])]), *returned, *([] if step else sums)],
            [array(rows, width)],
        )
        totals.append(total)
        if step:
            sums.append(swap(total, "local", 2 * step))
    return total


def solution(mesh):
    spread = ("parts", "node", "local")
    placed = (P(spread, None), P(spread, None), P(spread, None), P(None, spread), P(None, spread), P(spread, None))
    return jax.shard_map(
        per_device, mesh=mesh, in_specs=placed, out_specs=P(spread, None), check_vma=False
    )
```

```python
import functools

import jax
import jax.numpy as jnp
from jax import lax
from jax.experimental import pallas as pl
from jax.experimental.pallas import tpu as pltpu
from jax.sharding import PartitionSpec as P

LANES = 128
ORDER = [(2,), (3,), (1,), (0,)]
VMEM_BYTES, EXPERT_BYTES = 8 * 2**20, 26 * 2**20


def swap(value, axis, mask):
    pairs = [(source, source ^ mask) for source in range(lax.axis_size(axis))]
    return lax.ppermute(value, axis, pairs)


def after(value, earlier):
    if not earlier:
        return value
    return lax.optimization_barrier((value, *earlier))[0]


def together(moved, arrived):
    values = lax.optimization_barrier((*moved, *arrived[1:]))
    return values[: len(moved)], [arrived[0], *values[len(moved) :]]


def meta_of(ids, gates):
    parts = [ids]
    rest = gates
    for _ in range(3):
        piece = rest.astype(jnp.bfloat16).astype(jnp.float32)
        parts.append(piece)
        rest = rest - piece
    parts = jnp.concatenate(parts, axis=0).astype(jnp.bfloat16)
    count = parts.shape[0]
    same = lax.broadcasted_iota(jnp.int32, (count, LANES), 0) == lax.broadcasted_iota(jnp.int32, (count, LANES), 1)
    unit = jnp.where(same, 1.0, 0.0).astype(jnp.bfloat16)
    return lax.dot_general(parts, unit, (((0,), (0,)), ((), ())), preferred_element_type=jnp.float32)


def slots(place, meta, top, chain, capacity, count):
    meta = meta.astype(jnp.float32)
    rows = meta.shape[0]
    node, link = place[0], place[1]
    lane = lax.broadcasted_iota(jnp.int32, (rows, LANES), 1)
    expert = (jnp.bitwise_xor(lane, node) * chain + link).astype(jnp.float32)
    chosen = jnp.zeros((rows, LANES), jnp.float32)
    weight = jnp.zeros((rows, LANES), jnp.float32)
    for k in range(top):
        hit = meta[:, k : k + 1] == expert
        gate = meta[:, top + k : top + k + 1] + meta[:, 2 * top + k : 2 * top + k + 1]
        gate = gate + meta[:, 3 * top + k : 3 * top + k + 1]
        chosen = chosen + jnp.where(hit, 1.0, 0.0)
        weight = weight + jnp.where(hit, gate, 0.0)
    before = lax.broadcasted_iota(jnp.int32, (rows, rows), 0) > lax.broadcasted_iota(jnp.int32, (rows, rows), 1)
    rank = jnp.dot(
        jnp.where(before, 1.0, 0.0).astype(jnp.bfloat16),
        chosen.astype(jnp.bfloat16),
        preferred_element_type=jnp.float32,
    )
    rank = jnp.where(chosen > 0.5, rank, -1.0)
    slot = lax.broadcasted_iota(jnp.int32, (rows, capacity), 1).astype(jnp.float32)
    return [(jnp.where(rank[:, n : n + 1] == slot, 1.0, 0.0), weight[:, n : n + 1]) for n in range(count)]


def smem():
    return pl.BlockSpec(memory_space=pltpu.SMEM)


def vmem():
    return pl.BlockSpec(memory_space=pltpu.VMEM)


def call(kernel, name, place, inputs, outs, scratch=(), flops=0, stay=0):
    moved = sum(2 * v.size for v in inputs) + sum(2 * v.size for v in outs)
    return pl.pallas_call(
        kernel,
        out_shape=outs,
        in_specs=[smem()] + [vmem()] * (len(inputs) - stay) + [pl.BlockSpec(memory_space=pltpu.HBM)] * stay,
        out_specs=[vmem()] * len(outs),
        scratch_shapes=list(scratch),
        compiler_params=pltpu.CompilerParams(vmem_limit_bytes=EXPERT_BYTES if flops else VMEM_BYTES),
        cost_estimate=pl.CostEstimate(flops=flops, bytes_accessed=moved, transcendentals=0),
        name=name,
    )(place, *inputs)


def array(*shape):
    return jax.ShapeDtypeStruct(shape, jnp.bfloat16)


def pick(top, chain, capacity, place, meta, tokens, outs):
    for (hot, _), out in zip(slots(place, meta, top, chain, capacity, len(outs)), outs):
        rows = lax.dot_general(
            hot.astype(jnp.bfloat16), tokens, (((0,), (0,)), ((), ())), preferred_element_type=jnp.float32
        )
        out[...] = rows.astype(jnp.bfloat16)


def first_kernel(top, chain, capacity, place, tokens_from, routing_from, packed, *refs):
    outs, (tokens, routing, sems) = refs[:-3], refs[-3:]
    copies = [
        pltpu.make_async_copy(source, target, sems.at[i])
        for i, (source, target) in enumerate(((routing_from, routing), (tokens_from, tokens)))
    ]
    for copy in copies:
        copy.start()
    copies[0].wait()
    width = tokens.shape[1]
    meta = meta_of(routing[:top], routing[top:])
    packed[:, width:] = meta.astype(jnp.bfloat16)
    copies[1].wait()
    packed[:, :width] = tokens[...]
    pick(top, chain, capacity, place, meta, tokens[...], outs)


def select_kernel(top, chain, capacity, inputs, place, *refs):
    block, outs = refs[0][...], refs[inputs:]
    width = outs[0].shape[1]
    if inputs == 2:
        block = jnp.where(place[2] == 1, block, refs[1][...])
        kept, outs = outs[-1], outs[:-1]
        kept[...] = block
    pick(top, chain, capacity, place, block[:, width:], block[:, :width], outs)


def expert_kernel(capacity, count, place, *refs):
    rows, weights, outs = refs[:count], refs[count : count + 6], refs[count + 6 : 2 * count + 6]
    refs = refs[2 * count + 6 :]
    x, hidden, held, sems = refs[0], refs[1], [*weights[:3], *refs[2:5]], refs[5]
    cuts = 2
    copies = []
    for i, (source, target) in enumerate(zip(weights[3:], held[3:])):
        step = source.shape[0] // cuts
        copies.append(
            [
                pltpu.make_async_copy(
                    source.at[pl.ds(c * step, step)], target.at[pl.ds(c * step, step)], sems.at[i * cuts + c]
                )
                for c in range(cuts)
            ]
        )
    order = [copies[i][c] for c in range(cuts) for i in range(2)] + copies[2]
    for copy in order:
        copy.start()
    x[...] = jnp.concatenate([ref[...].astype(jnp.float32) for ref in rows], axis=0).astype(jnp.bfloat16)
    size = hidden.shape[1] // 2
    depth = x.shape[1] // 4
    for i in range(2):
        product = None
        for k in range(0, x.shape[1], depth):
            for c in range(cuts):
                if i == 1 and k == c * (x.shape[1] // cuts):
                    copies[0][c].wait()
                    copies[1][c].wait()
            both = jnp.concatenate([held[3 * i][k : k + depth, :], held[3 * i + 1][k : k + depth, :]], axis=1)
            term = jnp.dot(x[:, k : k + depth], both, preferred_element_type=jnp.float32)
            product = term if product is None else product + term
        gate, up = product[:, :size], product[:, size:]
        hidden[:, i * size : (i + 1) * size] = (gate / (1.0 + jnp.exp(-gate)) * up).astype(jnp.bfloat16)
    for copy in copies[2]:
        copy.wait()
    tile = 512
    for start in range(0, x.shape[1], tile):
        result = jnp.dot(hidden[:, :size], held[2][:, start : start + tile], preferred_element_type=jnp.float32)
        result += jnp.dot(hidden[:, size:], held[5][:, start : start + tile], preferred_element_type=jnp.float32)
        for n, out in enumerate(outs):
            out[:, start : start + tile] = result[n * capacity : (n + 1) * capacity].astype(jnp.bfloat16)


def weigh(pairs, values):
    total = None
    for (hot, weight), value in zip(pairs, values):
        scaled = hot * weight
        high = scaled.astype(jnp.bfloat16)
        low = (scaled - high.astype(jnp.float32)).astype(jnp.bfloat16)
        both = jnp.dot(jnp.concatenate([high, low], axis=0), value, preferred_element_type=jnp.float32)
        piece = both[: hot.shape[0]] + both[hot.shape[0] :]
        total = piece if total is None else total + piece
    return total


def combine_kernel(top, chain, capacity, count, place, block, *refs):
    results, others, out = refs[:count], refs[count:-1], refs[-1]
    width = out.shape[1]
    total = weigh(slots(place, block[:, width:], top, chain, capacity, count), [ref[...] for ref in results])
    for ref in others:
        total = total + ref[...].astype(jnp.float32)
    out[...] = total.astype(jnp.bfloat16)


def chain_pairs(pairs):
    return [(2 * source + core, 2 * target + core) for source, target in pairs for core in range(2)]


def per_device(tokens, expert_ids, gate_weights, w_gate, w_up, w_down):
    nodes = lax.axis_size("node")
    chain = lax.axis_size("local") // 2
    rows, top = expert_ids.shape
    width = tokens.shape[1]
    capacity = rows * top * 5 // (4 * nodes * chain)
    capacity = -(-capacity // 8) * 8
    spot = lax.axis_index("local") // 2
    middle = (spot == 1) | (spot == 2)
    place = jnp.stack([lax.axis_index("node"), spot, middle]).astype(jnp.int32)
    sizes = (top, chain, capacity)
    relay = chain == 4
    inner, outward, inward = [(1, 2), (2, 1)], [(1, 0), (2, 3)], [(0, 1), (3, 2)]
    hop = lambda value, pairs: lax.ppermute(value, "local", chain_pairs(pairs))
    send = lambda values: [values[0]] + [swap(values[n], "node", n) for n in range(1, nodes)]

    packed, *picked = call(
        functools.partial(first_kernel, *sizes),
        "first",
        place,
        [tokens, jnp.concatenate([expert_ids.T.astype(jnp.float32), gate_weights.T], axis=0)],
        [array(rows, width + LANES)] + [array(capacity, width)] * nodes,
        [
            pltpu.VMEM((rows, width), tokens.dtype),
            pltpu.VMEM((2 * top, rows), jnp.float32),
            pltpu.SemaphoreType.DMA((2,)),
        ],
        stay=2,
    )
    arrived = {0: send(picked)}
    own = (w_gate, w_up, w_down)
    other = [swap(w_gate, "local", 1)]
    blocks = [packed]

    def pick_for(step, *inputs):
        outs = [array(capacity, width)] * nodes + [array(*packed.shape)] * (len(inputs) - 1)
        picked = call(
            functools.partial(select_kernel, *sizes, len(inputs)), "select", place, list(inputs), outs
        )
        arrived[step] = send(picked[:nodes])
        blocks.append(picked[nodes] if len(inputs) > 1 else inputs[0])

    if relay:
        moved = [swap(packed, "local", 2), hop(after(packed, other), inner)]
        (first, third), arrived[0] = together(moved, arrived[0])
        pick_for(1, first)
        moved = [hop(first, inner), hop(third, outward)]
        moved, arrived[1] = together(moved, arrived[1])
        pick_for(2, *moved)
        other.append(swap(after(w_up, blocks[2:]), "local", 1))
        (last_hop, other[1]), arrived[2] = together([hop(blocks[2], outward), other[1]], arrived[2])
        pick_for(3, third, last_hop)
    else:
        for step in range(1, chain):
            pick_for(step, swap(packed, "local", 2 * step))
        other.append(swap(w_up, "local", 1))
    other.append(swap(after(w_down, [other[1], blocks[-1]]), "local", 1))

    def run(group):
        count = nodes * len(group)
        inputs = [value for step in group for value in arrived[step]]
        inputs[0] = after(inputs[0], last)
        outs = call(
            functools.partial(expert_kernel, capacity, count),
            "expert",
            place,
            [*inputs, *own, *other],
            [array(capacity, width)] * count,
            [
                pltpu.VMEM((count * capacity, width), jnp.bfloat16),
                pltpu.VMEM((count * capacity, 2 * w_gate.shape[1]), jnp.bfloat16),
            ]
            + [pltpu.VMEM(weight.shape, weight.dtype) for weight in own]
            + [pltpu.SemaphoreType.DMA((6,))],
            flops=12 * count * capacity * width * w_gate.shape[1],
            stay=3,
        )
        last[:] = [outs[0]]
        for i, step in enumerate(group):
            results[step] = outs[i * nodes : (i + 1) * nodes]

    results, last = {}, []
    for group in ORDER if relay else [(step,) for step in range(chain)]:
        run(group)
    sums, totals = [], []
    for step in reversed(range(chain)):
        ready = [*totals[:1], *(sums[:1] if step == 0 else [])] if step < chain - 2 else []
        result = results[step]
        returned = send([result[0]] + [after(value, ready) for value in result[1:]])
        (total,) = call(
            functools.partial(combine_kernel, *sizes, nodes),
            "combine",
            place,
            [after(blocks[step], [*totals[-1:], *(results[0][:1] if step == chain - 2 else [])]), *returned, *([] if step else sums)],
            [array(rows, width)],
        )
        totals.append(total)
        if step:
            sums.append(swap(total, "local", 2 * step))
    return total


def solution(mesh):
    spread = ("parts", "node", "local")
    placed = (P(spread, None), P(spread, None), P(spread, None), P(None, spread), P(None, spread), P(spread, None))
    return jax.shard_map(
        per_device, mesh=mesh, in_specs=placed, out_specs=P(spread, None), check_vma=False
    )
```
